256 devices in a mesh: pts: 128 (over x, y, z), ch: 2 (over core).
Axes of the slice: x: 4, y: 4, z: 8, core: 2. Of those that a mesh axis runs over, the one named last changes fastest.
Arguments:
- stream: bfloat16 [262144, 256], P('pts', 'ch'), may hold values from -6 to 6
- send_rows: int32 [2, 16384, 32], P(None, 'pts'), may hold values from -1 to 2047, as said below
- recv_slots: int32 [2, 262144], P(None, 'pts'), may hold values from 0 to 4095, as said below
- qkv_weight: bfloat16 [2, 256, 3, 256], P(None, None, None, 'ch'), as said below
- out_weight: bfloat16 [2, 256, 256], P(None, 'ch'), may hold values from -0.375 to 0.375
- up_weight: bfloat16 [2, 256, 1024], P(None, None, 'ch'), may hold values from -0.375 to 0.375
- down_weight: bfloat16 [2, 1024, 256], P(None, 'ch'), may hold values from -0.1875 to 0.1875
- gain_attn: float32 [2, 256], replicated, may hold values from 0.1 to 1.9
- gain_mlp: float32 [2, 256], replicated, may hold values from 0.1 to 1.9
Outputs:
- refined: bfloat16 [262144, 256], P('pts', 'ch')
The draws below stay inside these ranges and needn't reach their ends.
Inputs may be any that keep to these rules, and one draw needn't show every extreme that they name: For block b and devices s, d of pts, row s * N + d of send_rows lists the local rows of s that go to d, -1 marking an empty slot; at most 32 rows go from one device to one device, and some pair has exactly 32. The number of rows from s to s + o (cyclically) depends only on b and o. Each local row is sent once. recv_slots[b, d * 2048 + r] = s * 32 + j names a filled slot j of the rows that device d receives from device s; each filled slot is named once, so that the two tables make a permutation of all points. `qkv_weight`: projection weights, between -1.2 and 1.2; the query and key parts may be scaled so that scores reach a few hundred.
All inputs are finite; a program needn't handle non-finite values.
Results may differ from the reference program's by a relative error of at most 0.015.
Values may be sent and summed in bfloat16 or wider, within the bound.
No kernel may reach another device: no remote copies, remote signals or barrier semaphores. Data moves between devices by JAX's collectives and lax.ppermute only.
A program may use at most 64 MiB of HBM per device.

```python
import math
import jax
import jax.numpy as jnp
from jax import lax

D = 256
HEADS = 4
HEAD = 64
MLP_WIDTH = 1024
WIN = 1024
BLOCKS = 2
P_DEV = 2048
POINTS = 262144
CAP = 32
N_PTS = 128


def regroup_tables(key):
    group_rows = CAP // 4
    ngroups = P_DEV // group_rows
    shape_three = (N_PTS, ngroups, group_rows)
    send_list = []
    recv_list = []
    for layer_index in range(BLOCKS):
        layer_key = jax.random.fold_in(key, 100 + layer_index)
        coin_key, shift_key, src_key, dst_key = jax.random.split(layer_key, 4)
        group_ids = jnp.arange(ngroups, dtype=jnp.int32)
        coin_bits = jax.random.randint(coin_key, (ngroups,), 0, 2).astype(jnp.int32)
        coin_bits = jnp.where(group_ids < 4, 0, coin_bits)
        shift = jax.random.randint(shift_key, (), 0, N_PTS).astype(jnp.int32)
        offsets = (group_ids // 4 * 2 + coin_bits + shift) % N_PTS
        earlier = (offsets[None, :] == offsets[:, None]) & (group_ids[None, :] < group_ids[:, None])
        slot_rank = jnp.sum(earlier.astype(jnp.int32), axis=1)
        src_order = jax.vmap(lambda sub: jax.random.permutation(sub, P_DEV))(jax.random.split(src_key, N_PTS)).astype(jnp.int32)
        dst_order = jax.vmap(lambda sub: jax.random.permutation(sub, P_DEV))(jax.random.split(dst_key, N_PTS)).astype(jnp.int32)
        device_ids = jnp.arange(N_PTS, dtype=jnp.int32)[:, None, None]
        within = jnp.arange(group_rows, dtype=jnp.int32)[None, None, :]
        target = (device_ids + offsets[None, :, None]) % N_PTS
        slots = slot_rank[None, :, None] * group_rows + within
        sources = jnp.broadcast_to(device_ids, shape_three)
        send_table = jnp.full((N_PTS, N_PTS, CAP), -1, jnp.int32)
        send_table = send_table.at[sources, jnp.broadcast_to(target, shape_three), jnp.broadcast_to(slots, shape_three)].set(src_order.reshape(shape_three))
        anchor = (device_ids - offsets[None, :, None]) % N_PTS
        recv_value = jnp.broadcast_to(anchor * CAP + slots, shape_three)
        recv_table = jnp.zeros((N_PTS, P_DEV), jnp.int32)
        recv_table = recv_table.at[sources, dst_order.reshape(shape_three)].set(recv_value)
        send_list.append(send_table.reshape(N_PTS * N_PTS, CAP))
        recv_list.append(recv_table.reshape(N_PTS * P_DEV))
    return (jnp.stack(send_list), jnp.stack(recv_list))


def draw_send_rows(key, part):
    send_table, recv_table = regroup_tables(key)
    return send_table


def draw_recv_slots(key, part):
    send_table, recv_table = regroup_tables(key)
    return recv_table


def draw_qkv_weight(key, part):
    key = jax.random.fold_in(key, 7)
    normal_part = jnp.clip(jax.random.normal(key, (BLOCKS, D, 3, D), jnp.float32), -4.0, 4.0) * D ** (-0.5)
    return normal_part.astype(jnp.bfloat16)


def block_levels(stream_key, dims, cuts, least, high):
    loudness = 1.0
    for position, blocks in cuts:
        draws = jax.random.uniform(jax.random.fold_in(jax.random.fold_in(stream_key, 6), position), (blocks,), jnp.float32, least / len(cuts), high / len(cuts))
        loudness = loudness * jnp.repeat(jnp.exp(draws), dims[position] // blocks).reshape((-1,) + (1,) * (len(dims) - 1 - position))
    return loudness


def normal_values(rng, extent, deviation, most, cuts=(), kind=jnp.bfloat16):
    level = block_levels(rng, extent, cuts, -0.22, 0.18) if cuts else 1.0
    values = jax.random.normal(rng, extent, jnp.float32) * deviation * level
    return jnp.minimum(jnp.maximum(values, -most), most).astype(kind)


def setup_inputs(seed: int = 0) -> dict:
    keys = jax.random.split(jax.random.key(seed), 10)
    stream = normal_values(keys[0], (POINTS, D), 1.0, 6.0, ((0, 128), (1, 2)))
    send_rows = draw_send_rows(jax.random.fold_in(keys[9], 71), 0)
    recv_slots = draw_recv_slots(jax.random.fold_in(keys[9], 71), 0)
    qkv_weight = draw_qkv_weight(jax.random.fold_in(keys[9], 71), 0)
    out_weight = normal_values(keys[4], (BLOCKS, D, D), D ** -0.5, 0.375, ((1, 2),))
    up_weight = normal_values(keys[5], (BLOCKS, D, MLP_WIDTH), D ** -0.5, 0.375, ((2, 2),))
    down_weight = normal_values(keys[6], (BLOCKS, MLP_WIDTH, D), MLP_WIDTH ** -0.5, 0.1875, ((1, 2),))
    gain_attn = jnp.clip(1.0 + 0.18 * jax.random.normal(keys[7], (BLOCKS, D), jnp.float32), 0.1, 1.9)
    gain_mlp = jnp.clip(1.0 + 0.18 * jax.random.normal(keys[8], (BLOCKS, D), jnp.float32), 0.1, 1.9)
    return {"stream": stream, "send_rows": send_rows, "recv_slots": recv_slots, "qkv_weight": qkv_weight, "out_weight": out_weight, "up_weight": up_weight, "down_weight": down_weight, "gain_attn": gain_attn, "gain_mlp": gain_mlp}


def layer_norm(values, gain):
    average = lax.optimization_barrier(jnp.mean(values, axis=-1, keepdims=True))
    centred = values - average
    spread = lax.optimization_barrier(jnp.mean(centred * centred, axis=-1, keepdims=True))
    return centred * lax.rsqrt(spread + 1e-05) * gain

def source_rows(send_table, recv_table):
    slot_index = recv_table
    source = slot_index // CAP
    within = slot_index % CAP
    target = jnp.arange(POINTS, dtype=jnp.int32) // P_DEV
    local_row = send_table[source * N_PTS + target, within]
    return (source * P_DEV + local_row).astype(jnp.int32)

def window_block(current, qkv_w, out_w, up_w, down_w, gain_a, gain_m):
    normed = layer_norm(current.astype(jnp.float32), gain_a).astype(jnp.bfloat16)
    projected = jnp.dot(normed, qkv_w.reshape(D, 3 * D), preferred_element_type=jnp.float32)
    projected = projected.astype(jnp.bfloat16).reshape(WIN, 3, HEADS, HEAD)
    query_rows = projected[:, 0].astype(jnp.float32)
    key_rows = projected[:, 1].astype(jnp.float32)
    value_rows = projected[:, 2].astype(jnp.float32)
    scores = jnp.einsum('qhd,khd->hqk', query_rows, key_rows) / math.sqrt(HEAD)
    weights = jax.nn.softmax(scores, axis=-1).astype(jnp.bfloat16)
    attended = jnp.einsum('hqk,khd->qhd', weights.astype(jnp.float32), value_rows)
    attended = attended.astype(jnp.bfloat16).reshape(WIN, D)
    hstream = (current.astype(jnp.float32) + jnp.dot(attended, out_w, preferred_element_type=jnp.float32)).astype(jnp.bfloat16)
    normed_two = layer_norm(hstream.astype(jnp.float32), gain_m).astype(jnp.bfloat16)
    hidden_act = jax.nn.gelu(jnp.dot(normed_two, up_w, preferred_element_type=jnp.float32)).astype(jnp.bfloat16)
    result = hstream.astype(jnp.float32) + jnp.dot(hidden_act, down_w, preferred_element_type=jnp.float32)
    return result.astype(jnp.bfloat16)

def reference(stream, send_rows, recv_slots, qkv_weight, out_weight, up_weight, down_weight, gain_attn, gain_mlp):
    for layer_index in range(BLOCKS):
        stream = stream[source_rows(send_rows[layer_index], recv_slots[layer_index])]
        windows = stream.reshape(POINTS // WIN, WIN, D)

        def one_window(window_rows, layer_index=layer_index):
            return window_block(window_rows, qkv_weight[layer_index], out_weight[layer_index], up_weight[layer_index], down_weight[layer_index], gain_attn[layer_index], gain_mlp[layer_index])
        stream = lax.map(one_window, windows).reshape(POINTS, D)
    return stream
```

```python
import math

import jax
import jax.numpy as jnp
from jax import lax
from jax.experimental import pallas as pl
from jax.experimental.pallas import tpu as pltpu
from jax.sharding import PartitionSpec as P

D = 256
HALF = 128
HEAD = 64
WIN = 1024
BLOCKS = 2
SWAP = [(0, 1), (1, 0)]
LANES = 128
ROW_TILE = 512
QUERY_TILE = 256
VMEM = 40 * 1024 * 1024


def swap(value):
    return lax.ppermute(value, "ch", SWAP)


def one_hot_rows(index_row, depth):
    count = index_row.shape[1]
    wide = jnp.concatenate(
        [
            jnp.transpose(jnp.broadcast_to(index_row[:, at : at + LANES], (LANES, LANES)))
            for at in range(0, count, LANES)
        ],
        axis=0,
    )
    block = jnp.right_shift(wide, 7)
    inner = jnp.bitwise_and(wide, LANES - 1)
    lane = lax.broadcasted_iota(jnp.int32, (count, LANES), 1)
    base = jnp.where(inner == lane, 1.0, 0.0).astype(jnp.bfloat16)
    block = block.astype(jnp.float32).astype(jnp.bfloat16)
    zero = jnp.zeros_like(base)
    return jnp.concatenate(
        [jnp.where(block == k, base, zero) for k in range(depth // LANES)], axis=1
    )


def pick_kernel(index_ref, *refs):
    sources, out_ref = refs[:-1], refs[-1]
    total = None
    width = sources[0].shape[0]
    hot = one_hot_rows(index_ref[0], width * len(sources))
    for n, source in enumerate(sources):
        part = jnp.dot(
            hot[:, n * width : (n + 1) * width], source[...], preferred_element_type=jnp.float32
        )
        total = part if total is None else total + part
    out_ref[...] = total.astype(jnp.bfloat16)


def pick(index, *sources):
    count = index.size
    depth = sum(source.shape[0] for source in sources)
    steps = count // ROW_TILE
    return pl.pallas_call(
        pick_kernel,
        grid=(steps,),
        in_specs=[pl.BlockSpec((1, 1, ROW_TILE), lambda i: (i, 0, 0))]
        + [pl.BlockSpec(source.shape, lambda i: (0, 0)) for source in sources],
        out_specs=pl.BlockSpec((ROW_TILE, HALF), lambda i: (i, 0)),
        out_shape=jax.ShapeDtypeStruct((count, HALF), jnp.bfloat16),
        compiler_params=pltpu.CompilerParams(vmem_limit_bytes=VMEM),
        cost_estimate=pl.CostEstimate(
            flops=4 * count * depth * HALF, bytes_accessed=(count + depth) * 256, transcendentals=0
        ),
    )(index.reshape(steps, 1, ROW_TILE), *sources)


def layer_norm(values, gain):
    average = jnp.mean(values, axis=-1, keepdims=True)
    centred = values - average
    spread = jnp.mean(centred * centred, axis=-1, keepdims=True)
    return centred * lax.rsqrt(spread + 1e-05) * gain


def gelu(x):
    inner = x * (math.sqrt(2 / math.pi) + (math.sqrt(2 / math.pi) * 0.044715) * (x * x))
    half = 0.5 * x
    return half + half * jnp.tanh(inner)


def block_kernel(
    core_ref,
    mine_ref,
    got_ref,
    qkv_a,
    qkv_b,
    out_a,
    out_b,
    up_a,
    up_b,
    down_a,
    down_b,
    gain_a,
    gain_m,
    keep_ref,
    give_ref,
    proj_ref,
    attended_ref,
):
    first = core_ref[0] == 0
    mine, got = mine_ref[...], got_ref[...]
    low = jnp.where(first, mine, got)
    high = jnp.where(first, got, mine)
    current = jnp.concatenate([low, high], axis=1)
    normed = layer_norm(current.astype(jnp.float32), gain_a[...]).astype(jnp.bfloat16)
    for n, weight in enumerate((qkv_a, qkv_b)):
        proj_ref[n] = jnp.dot(normed, weight[...], preferred_element_type=jnp.float32).astype(
            jnp.bfloat16
        )
    factor = math.log2(math.e) / math.sqrt(HEAD)
    for n in range(2):
        keys = proj_ref[n, :, HALF : 2 * HALF]
        values = proj_ref[n, :, 2 * HALF :]
        low_wide = lax.broadcasted_iota(jnp.int32, (WIN, HALF), 1) < HEAD
        one = jnp.ones_like(values)
        rights = (jnp.where(low_wide, values, one), jnp.where(low_wide, one, values))
        for at in range(0, WIN, QUERY_TILE):
            query = proj_ref[n, at : at + QUERY_TILE, :HALF]
            low_lane = lax.broadcasted_iota(jnp.int32, (QUERY_TILE, HALF), 1) < HEAD
            zero = jnp.zeros_like(query)
            lefts = (jnp.where(low_lane, query, zero), jnp.where(low_lane, zero, query))
            sums = []
            for left, right in zip(lefts, rights):
                scores = lax.dot_general(
                    left, keys, (((1,), (1,)), ((), ())), preferred_element_type=jnp.float32
                )
                top = jnp.max(scores, axis=1, keepdims=True)
                weights = jnp.exp2((scores - top) * factor).astype(jnp.bfloat16)
                sums.append(jnp.dot(weights, right, preferred_element_type=jnp.float32))
            top_part = jnp.where(low_lane, sums[0], sums[1])
            bottom = jnp.where(
                low_lane, pltpu.roll(sums[0], HEAD, 1), pltpu.roll(sums[1], HEAD, 1)
            )
            attended_ref[n, at : at + QUERY_TILE, :] = (top_part / bottom).astype(jnp.bfloat16)
    added = jnp.dot(attended_ref[0], out_a[...], preferred_element_type=jnp.float32) + jnp.dot(
        attended_ref[1], out_b[...], preferred_element_type=jnp.float32
    )
    hstream = (current.astype(jnp.float32) + added).astype(jnp.bfloat16)
    normed_two = layer_norm(hstream.astype(jnp.float32), gain_m[...]).astype(jnp.bfloat16)
    result = hstream.astype(jnp.float32)
    for up, down in ((up_a, down_a), (up_b, down_b)):
        hidden = gelu(jnp.dot(normed_two, up[...], preferred_element_type=jnp.float32))
        result = result + jnp.dot(
            hidden.astype(jnp.bfloat16), down[...], preferred_element_type=jnp.float32
        )
    result = result.astype(jnp.bfloat16)
    low, high = result[:, :HALF], result[:, HALF:]
    keep_ref[...] = jnp.where(first, low, high)
    give_ref[...] = jnp.where(first, high, low)


def window_block(core, mine, got, weights, gain_attn, gain_mlp):
    half = jax.ShapeDtypeStruct((WIN, HALF), jnp.bfloat16)
    whole = pl.BlockSpec(memory_space=pltpu.VMEM)
    return pl.pallas_call(
        block_kernel,
        in_specs=[pl.BlockSpec(memory_space=pltpu.SMEM)] + [whole] * (4 + len(weights)),
        out_specs=[whole, whole],
        out_shape=[half, half],
        scratch_shapes=[
            pltpu.VMEM((2, WIN, 3 * HALF), jnp.bfloat16),
            pltpu.VMEM((2, WIN, HALF), jnp.bfloat16),
        ],
        compiler_params=pltpu.CompilerParams(vmem_limit_bytes=VMEM),
        cost_estimate=pl.CostEstimate(
            flops=6_000_000_000, bytes_accessed=3_000_000, transcendentals=5_000_000
        ),
    )(core, mine, got, *weights, gain_attn, gain_mlp)


def shards(
    stream,
    send_rows,
    recv_slots,
    qkv_weight,
    out_weight,
    up_weight,
    down_weight,
    gain_attn,
    gain_mlp,
):
    core = lax.axis_index("ch")
    core_word = core.astype(jnp.int32).reshape(1)
    qkv = qkv_weight.reshape(BLOCKS, D, 3 * HALF)
    owned = (qkv, out_weight, up_weight, down_weight)
    fetched = tuple(swap(array) for array in owned)
    sources = (stream,)
    flip = 0
    for layer in range(BLOCKS):
        index = jnp.maximum(send_rows[layer], 0) ^ flip
        picked = pick(index, *sources)
        moved = lax.all_to_all(
            picked.reshape(-1, 32, HALF), "pts", split_axis=0, concat_axis=0, tiled=True
        ).reshape(-1, HALF)
        slots = recv_slots[layer].reshape(2, WIN)
        theirs = lax.dynamic_index_in_dim(slots, 1 - core, 0, keepdims=False)
        ours = lax.dynamic_index_in_dim(slots, core, 0, keepdims=False)
        got = swap(pick(theirs, moved))
        mine = pick(ours, moved)
        weights = []
        for own, other in zip(owned, fetched):
            weights += [own[layer], other[layer]]
        keep, give = window_block(
            core_word, mine, got, weights, gain_attn[layer : layer + 1], gain_mlp[layer : layer + 1]
        )
        back = swap(give)
        sources = (keep, back)
        flip = core * WIN
    result = jnp.zeros((2 * WIN, HALF), jnp.bfloat16)
    result = lax.dynamic_update_slice(result, keep, (core * WIN, 0))
    return lax.dynamic_update_slice(result, back, ((1 - core) * WIN, 0))


def solution(mesh):
    in_specs = (
        P("pts", "ch"),
        P(None, "pts", None),
        P(None, "pts"),
        P(None, None, None, "ch"),
        P(None, "ch", None),
        P(None, None, "ch"),
        P(None, "ch", None),
        P(),
        P(),
    )
    out_specs = P("pts", "ch")
    return jax.shard_map(shards, mesh=mesh, in_specs=in_specs, out_specs=out_specs, check_vma=False)
```

```python
import math

import jax
import jax.numpy as jnp
from jax import lax
from jax.experimental import pallas as pl
from jax.experimental.pallas import tpu as pltpu
from jax.sharding import PartitionSpec as P

D = 256
HALF = 128
HEAD = 64
WIN = 1024
BLOCKS = 2
SWAP = [(0, 1), (1, 0)]
QUERY_TILE = 1024
VMEM = 40 * 1024 * 1024


def swap(value):
    return lax.ppermute(value, "ch", SWAP)


def pick_kernel(index_ref, *refs):
    sources, out_ref = refs[:-1], refs[-1]
    index = index_ref[0].astype(jnp.int16)
    total = None
    start = 0
    for source in sources:
        shape = (source.shape[0], index.shape[1])
        row = lax.broadcasted_iota(jnp.int16, shape, 0) + jnp.int16(start)
        hot = jnp.where(
            jnp.broadcast_to(index, shape) == row,
            jnp.ones(shape, jnp.bfloat16),
            jnp.zeros(shape, jnp.bfloat16),
        )
        part = lax.dot_general(
            source[...], hot, (((0,), (0,)), ((), ())), preferred_element_type=jnp.float32
        )
        total = part if total is None else total + part
        start += shape[0]
    out_ref[...] = total.T.astype(jnp.bfloat16)


def pick(index, *sources):
    count = index.size
    depth = sum(source.shape[0] for source in sources)
    tile = min(count, 2048)
    steps = count // tile
    return pl.pallas_call(
        pick_kernel,
        grid=(steps,),
        in_specs=[pl.BlockSpec((1, 1, tile), lambda i: (i, 0, 0))]
        + [pl.BlockSpec(source.shape, lambda i: (0, 0)) for source in sources],
        out_specs=pl.BlockSpec((tile, HALF), lambda i: (i, 0)),
        out_shape=jax.ShapeDtypeStruct((count, HALF), jnp.bfloat16),
        compiler_params=pltpu.CompilerParams(vmem_limit_bytes=VMEM),
        cost_estimate=pl.CostEstimate(
            flops=4 * count * depth * HALF, bytes_accessed=(count + depth) * 256, transcendentals=0
        ),
    )(index.reshape(steps, 1, tile), *sources)


def layer_norm(values, gain):
    average = jnp.mean(values, axis=-1, keepdims=True)
    centred = values - average
    spread = jnp.mean(centred * centred, axis=-1, keepdims=True)
    return centred * lax.rsqrt(spread + 1e-05) * gain


def gelu(x):
    inner = x * (math.sqrt(2 / math.pi) + (math.sqrt(2 / math.pi) * 0.044715) * (x * x))
    half = 0.5 * x
    return half + half * jnp.tanh(inner)


def block_kernel(
    core_ref,
    mine_ref,
    got_ref,
    qkv_a,
    qkv_b,
    out_a,
    out_b,
    up_a,
    up_b,
    down_a,
    down_b,
    gain_a,
    gain_m,
    keep_ref,
    give_ref,
    attended_ref,
):
    first = core_ref[0] == 0
    mine, got = mine_ref[...], got_ref[...]
    low = jnp.where(first, mine, got)
    high = jnp.where(first, got, mine)
    current = jnp.concatenate([low, high], axis=1)
    normed = layer_norm(current.astype(jnp.float32), gain_a[...]).astype(jnp.bfloat16)
    factor = math.log2(math.e) / math.sqrt(HEAD)
    over_rows = (((0,), (1,)), ((), ()))
    units = []
    for n, weight in enumerate((qkv_a, qkv_b)):
        queries = lax.dot_general(
            weight[:, :HALF], normed, over_rows, preferred_element_type=jnp.float32
        ).astype(jnp.bfloat16)
        keys = jnp.dot(
            normed, weight[:, HALF : 2 * HALF], preferred_element_type=jnp.float32
        ).astype(jnp.bfloat16)
        values = lax.dot_general(
            weight[:, 2 * HALF :], normed, over_rows, preferred_element_type=jnp.float32
        ).astype(jnp.bfloat16)
        zero = jnp.zeros((HEAD, WIN), jnp.bfloat16)
        ones = jnp.ones((16, WIN), jnp.bfloat16)
        for h in range(2):
            rows = slice(h * HEAD, (h + 1) * HEAD)
            pair = [zero, zero]
            pair[h] = queries[rows]
            query = jnp.concatenate(pair, axis=0)
            value = jnp.concatenate([values[rows], ones], axis=0)
            for at in range(0, WIN, QUERY_TILE):
                units.append((keys, query[:, at : at + QUERY_TILE], value, n * HALF + h * HEAD, at))

    def score(unit):
        return jnp.dot(unit[0], unit[1], preferred_element_type=jnp.float32)

    def finish(unit, scores):
        top = jnp.max(scores, axis=0, keepdims=True)
        weights = jnp.exp2((scores - top) * factor).astype(jnp.bfloat16)
        sums = jnp.dot(unit[2], weights, preferred_element_type=jnp.float32)
        attended_ref[unit[3] : unit[3] + HEAD, unit[4] : unit[4] + QUERY_TILE] = (
            sums[:HEAD] / sums[HEAD : HEAD + 1]
        ).astype(jnp.bfloat16)

    ahead = score(units[0])
    for i, unit in enumerate(units):
        now, ahead = ahead, (score(units[i + 1]) if i + 1 < len(units) else None)
        finish(unit, now)
    out_weight = jnp.concatenate([out_a[...], out_b[...]], axis=0)
    added = lax.dot_general(
        attended_ref[...], out_weight, (((0,), (0,)), ((), ())), preferred_element_type=jnp.float32
    )
    hstream = (current.astype(jnp.float32) + added).astype(jnp.bfloat16)
    normed_two = layer_norm(hstream.astype(jnp.float32), gain_m[...]).astype(jnp.bfloat16)
    result = hstream.astype(jnp.float32)
    for up, down in ((up_a, down_a), (up_b, down_b)):
        hidden = gelu(jnp.dot(normed_two, up[...], preferred_element_type=jnp.float32))
        result = result + jnp.dot(
            hidden.astype(jnp.bfloat16), down[...], preferred_element_type=jnp.float32
        )
    result = result.astype(jnp.bfloat16)
    low, high = result[:, :HALF], result[:, HALF:]
    keep_ref[...] = jnp.where(first, low, high)
    give_ref[...] = jnp.where(first, high, low)


def window_block(core, mine, got, weights, gain_attn, gain_mlp):
    half = jax.ShapeDtypeStruct((WIN, HALF), jnp.bfloat16)
    whole = pl.BlockSpec(memory_space=pltpu.VMEM)
    return pl.pallas_call(
        block_kernel,
        in_specs=[pl.BlockSpec(memory_space=pltpu.SMEM)] + [whole] * (4 + len(weights)),
        out_specs=[whole, whole],
        out_shape=[half, half],
        scratch_shapes=[
            pltpu.VMEM((D, WIN), jnp.bfloat16),
        ],
        compiler_params=pltpu.CompilerParams(vmem_limit_bytes=VMEM),
        cost_estimate=pl.CostEstimate(
            flops=6_000_000_000, bytes_accessed=3_000_000, transcendentals=5_000_000
        ),
    )(core, mine, got, *weights, gain_attn, gain_mlp)


def shards(
    stream,
    send_rows,
    recv_slots,
    qkv_weight,
    out_weight,
    up_weight,
    down_weight,
    gain_attn,
    gain_mlp,
):
    core = lax.axis_index("ch")
    core_word = core.astype(jnp.int32).reshape(1)
    qkv = qkv_weight.reshape(BLOCKS, D, 3 * HALF)
    owned = (qkv, out_weight, up_weight, down_weight)
    fetched = tuple(swap(array) for array in owned)
    sources = (stream,)
    flip = 0
    for layer in range(BLOCKS):
        index = jnp.maximum(send_rows[layer], 0) ^ flip
        picked = pick(index, *sources)
        moved = lax.all_to_all(
            picked.reshape(-1, 32, HALF), "pts", split_axis=0, concat_axis=0, tiled=True
        ).reshape(-1, HALF)
        slots = recv_slots[layer].reshape(2, WIN)
        theirs = lax.dynamic_index_in_dim(slots, 1 - core, 0, keepdims=False)
        ours = lax.dynamic_index_in_dim(slots, core, 0, keepdims=False)
        got = swap(pick(theirs, moved))
        mine = pick(ours, moved)
        weights = []
        for own, other in zip(owned, fetched):
            weights += [own[layer], other[layer]]
        keep, give = window_block(
            core_word, mine, got, weights, gain_attn[layer : layer + 1], gain_mlp[layer : layer + 1]
        )
        back = swap(give)
        sources = (keep, back)
        flip = core * WIN
    result = jnp.zeros((2 * WIN, HALF), jnp.bfloat16)
    result = lax.dynamic_update_slice(result, keep, (core * WIN, 0))
    return lax.dynamic_update_slice(result, back, ((1 - core) * WIN, 0))


def solution(mesh):
    in_specs = (
        P("pts", "ch"),
        P(None, "pts", None),
        P(None, "pts"),
        P(None, None, None, "ch"),
        P(None, "ch", None),
        P(None, None, "ch"),
        P(None, "ch", None),
        P(),
        P(),
    )
    out_specs = P("pts", "ch")
    return jax.shard_map(shards, mesh=mesh, in_specs=in_specs, out_specs=out_specs, check_vma=False)
```

```python
import functools
import math

import jax
import jax.numpy as jnp
from jax import lax
from jax.experimental import pallas as pl
from jax.experimental.pallas import tpu as pltpu
from jax.sharding import PartitionSpec as P

D = 256
HALF = 128
HEAD = 64
WIN = 1024
BLOCKS = 2
SWAP = [(0, 1), (1, 0)]
QUERY_TILE = 1024
VMEM = 40 * 1024 * 1024


def swap(value):
    return lax.ppermute(value, "ch", SWAP)


def pick_kernel(flips, core_ref, index_ref, *refs):
    sources, out_ref = refs[:-1], refs[-1]
    index = index_ref[0, 0]
    if flips:
        index = jnp.bitwise_xor(index, core_ref[0] * WIN)
    index = index.astype(jnp.int16)
    total = None
    start = 0
    for source in sources:
        shape = (source.shape[0], index.shape[1])
        row = lax.broadcasted_iota(jnp.int16, shape, 0) + jnp.int16(start)
        hot = jnp.where(
            jnp.broadcast_to(index, shape) == row,
            jnp.ones(shape, jnp.bfloat16),
            jnp.zeros(shape, jnp.bfloat16),
        )
        part = lax.dot_general(
            source[...], hot, (((0,), (0,)), ((), ())), preferred_element_type=jnp.float32
        )
        total = part if total is None else total + part
        start += shape[0]
    out_ref[...] = total.T.astype(jnp.bfloat16)


def pick(core, table, layer, part, *sources, flips=False):
    tile = table.shape[3]
    steps = table.shape[1] if part is None else 1
    depth = sum(source.shape[0] for source in sources)

    def block(i, word):
        return (layer, i if part is None else part(word[0]), 0, 0)

    return pl.pallas_call(
        functools.partial(pick_kernel, flips),
        grid_spec=pltpu.PrefetchScalarGridSpec(
            num_scalar_prefetch=1,
            grid=(steps,),
            in_specs=[pl.BlockSpec((1, 1, 1, tile), block)]
            + [pl.BlockSpec(source.shape, lambda i, word: (0, 0)) for source in sources],
            out_specs=pl.BlockSpec((tile, HALF), lambda i, word: (i, 0)),
        ),
        out_shape=jax.ShapeDtypeStruct((steps * tile, HALF), jnp.bfloat16),
        compiler_params=pltpu.CompilerParams(vmem_limit_bytes=VMEM),
        cost_estimate=pl.CostEstimate(
            flops=4 * steps * tile * depth * HALF,
            bytes_accessed=(steps * tile + depth) * 256,
            transcendentals=0,
        ),
    )(core, table, *sources)


def layer_norm(values, gain):
    average = jnp.mean(values, axis=-1, keepdims=True)
    centred = values - average
    spread = jnp.mean(centred * centred, axis=-1, keepdims=True)
    return centred * lax.rsqrt(spread + 1e-05) * gain


def gelu(x):
    inner = x * (math.sqrt(2 / math.pi) + (math.sqrt(2 / math.pi) * 0.044715) * (x * x))
    half = 0.5 * x
    return half + half * jnp.tanh(inner)


def block_kernel(
    layer,
    core_ref,
    mine_ref,
    got_ref,
    qkv_a,
    qkv_b,
    out_a,
    out_b,
    up_a,
    up_b,
    down_a,
    down_b,
    gain_a,
    gain_m,
    keep_ref,
    give_ref,
    attended_ref,
):
    first = core_ref[0] == 0
    mine, got = mine_ref[...], got_ref[...]
    low = jnp.where(first, mine, got)
    high = jnp.where(first, got, mine)
    current = jnp.concatenate([low, high], axis=1)
    normed = layer_norm(current.astype(jnp.float32), gain_a[layer : layer + 1]).astype(jnp.bfloat16)
    factor = math.log2(math.e) / math.sqrt(HEAD)
    over_rows = (((0,), (1,)), ((), ()))
    units = []
    for n, weight in enumerate((qkv_a, qkv_b)):
        queries = lax.dot_general(
            weight[layer, 0], normed, over_rows, preferred_element_type=jnp.float32
        ).astype(jnp.bfloat16)
        keys = jnp.dot(
            normed, weight[layer, 1], preferred_element_type=jnp.float32
        ).astype(jnp.bfloat16)
        values = lax.dot_general(
            weight[layer, 2], normed, over_rows, preferred_element_type=jnp.float32
        ).astype(jnp.bfloat16)
        zero = jnp.zeros((HEAD, WIN), jnp.bfloat16)
        ones = jnp.ones((16, WIN), jnp.bfloat16)
        for h in range(2):
            rows = slice(h * HEAD, (h + 1) * HEAD)
            pair = [zero, zero]
            pair[h] = queries[rows]
            query = jnp.concatenate(pair, axis=0)
            value = jnp.concatenate([values[rows], ones], axis=0)
            for at in range(0, WIN, QUERY_TILE):
                units.append((keys, query[:, at : at + QUERY_TILE], value, n * HALF + h * HEAD, at))

    def score(unit):
        return jnp.dot(unit[0], unit[1], preferred_element_type=jnp.float32)

    def finish(unit, scores):
        top = jnp.max(scores, axis=0, keepdims=True)
        weights = jnp.exp2((scores - top) * factor).astype(jnp.bfloat16)
        sums = jnp.dot(unit[2], weights, preferred_element_type=jnp.float32)
        attended_ref[unit[3] : unit[3] + HEAD, unit[4] : unit[4] + QUERY_TILE] = (
            sums[:HEAD] / sums[HEAD : HEAD + 1]
        ).astype(jnp.bfloat16)

    ahead = score(units[0])
    for i, unit in enumerate(units):
        now, ahead = ahead, (score(units[i + 1]) if i + 1 < len(units) else None)
        finish(unit, now)
    out_weight = jnp.concatenate([out_a[layer], out_b[layer]], axis=0)
    added = lax.dot_general(
        attended_ref[...], out_weight, (((0,), (0,)), ((), ())), preferred_element_type=jnp.float32
    )
    hstream = (current.astype(jnp.float32) + added).astype(jnp.bfloat16)
    normed_two = layer_norm(hstream.astype(jnp.float32), gain_m[layer : layer + 1]).astype(jnp.bfloat16)
    result = hstream.astype(jnp.float32)
    for up, down in ((up_a, down_a), (up_b, down_b)):
        hidden = gelu(jnp.dot(normed_two, up[layer], preferred_element_type=jnp.float32))
        result = result + jnp.dot(
            hidden.astype(jnp.bfloat16), down[layer], preferred_element_type=jnp.float32
        )
    result = result.astype(jnp.bfloat16)
    low, high = result[:, :HALF], result[:, HALF:]
    kept = jnp.where(first, low, high)
    if keep_ref.shape[0] == WIN:
        keep_ref[...] = kept
    else:
        keep_ref[pl.ds(pl.multiple_of(core_ref[0] * WIN, WIN), WIN), :] = kept
    give_ref[...] = jnp.where(first, high, low)


def window_block(layer, core, mine, got, weights, gain_attn, gain_mlp):
    kept = WIN if layer + 1 < BLOCKS else 2 * WIN
    whole = pl.BlockSpec(memory_space=pltpu.VMEM)
    return pl.pallas_call(
        functools.partial(block_kernel, layer),
        in_specs=[pl.BlockSpec(memory_space=pltpu.SMEM)] + [whole] * (4 + len(weights)),
        out_specs=[whole, whole],
        out_shape=[
            jax.ShapeDtypeStruct((kept, HALF), jnp.bfloat16),
            jax.ShapeDtypeStruct((WIN, HALF), jnp.bfloat16),
        ],
        scratch_shapes=[
            pltpu.VMEM((D, WIN), jnp.bfloat16),
        ],
        compiler_params=pltpu.CompilerParams(vmem_limit_bytes=VMEM),
        cost_estimate=pl.CostEstimate(
            flops=6_000_000_000, bytes_accessed=3_000_000, transcendentals=5_000_000
        ),
    )(core, mine, got, *weights, gain_attn, gain_mlp)


def shards(
    stream,
    send_rows,
    recv_slots,
    qkv_weight,
    out_weight,
    up_weight,
    down_weight,
    gain_attn,
    gain_mlp,
):
    core = lax.axis_index("ch").astype(jnp.int32)
    word = core.reshape(1)
    weights = []
    for array in (qkv_weight.transpose(0, 2, 1, 3), out_weight, up_weight, down_weight):
        weights += [array, swap(array)]
    send_table = send_rows.reshape(BLOCKS, 2, 1, -1)
    recv_table = recv_slots.reshape(BLOCKS, 2, 1, WIN)
    sources = (stream,)
    for layer in range(BLOCKS):
        picked = pick(word, send_table, layer, None, *sources, flips=layer > 0)
        moved = lax.all_to_all(
            picked.reshape(-1, 32, HALF), "pts", split_axis=0, concat_axis=0, tiled=True
        ).reshape(-1, HALF)
        got = swap(pick(word, recv_table, layer, lambda own: 1 - own, moved))
        mine = pick(word, recv_table, layer, lambda own: own, moved)
        keep, give = window_block(layer, word, mine, got, weights, gain_attn, gain_mlp)
        back = swap(give)
        sources = (keep, back)
    return lax.dynamic_update_slice(keep, back, ((1 - core) * WIN, 0))


def solution(mesh):
    in_specs = (
        P("pts", "ch"),
        P(None, "pts", None),
        P(None, "pts"),
        P(None, None, None, "ch"),
        P(None, "ch", None),
        P(None, None, "ch"),
        P(None, "ch", None),
        P(),
        P(),
    )
    out_specs = P("pts", "ch")
    return jax.shard_map(shards, mesh=mesh, in_specs=in_specs, out_specs=out_specs, check_vma=False)
```

```python
import functools
import math

import jax
import jax.numpy as jnp
from jax import lax
from jax.experimental import pallas as pl
from jax.experimental.pallas import tpu as pltpu
from jax.sharding import PartitionSpec as P

D = 256
HALF = 128
HEAD = 64
WIN = 1024
BLOCKS = 2
SWAP = [(0, 1), (1, 0)]
QUERY_TILE = 1024
VMEM = 40 * 1024 * 1024


def swap(value):
    return lax.ppermute(value, "ch", SWAP)


def pick_kernel(flips, start, core_ref, index_ref, source_ref, *refs):
    out_ref = refs[-1]
    index = index_ref[0, 0]
    if flips:
        index = jnp.bitwise_xor(index, core_ref[0] * WIN)
    index = index.astype(jnp.int16)
    shape = (source_ref.shape[0], index.shape[1])
    row = lax.broadcasted_iota(jnp.int16, shape, 0) + jnp.int16(start)
    hot = jnp.where(
        jnp.broadcast_to(index, shape) == row,
        jnp.ones(shape, jnp.bfloat16),
        jnp.zeros(shape, jnp.bfloat16),
    )
    found = lax.dot_general(
        source_ref[...], hot, (((0,), (0,)), ((), ())), preferred_element_type=jnp.float32
    )
    found = found.T.astype(jnp.bfloat16)
    out_ref[...] = found if len(refs) == 1 else found + refs[0][...]


def pick(core, table, layer, part, source, others=None, start=0, flips=False):
    tile = table.shape[3]
    steps = table.shape[1] if part is None else 1
    depth = source.shape[0]
    rows = pl.BlockSpec((tile, HALF), lambda i, word: (i, 0))

    def block(i, word):
        return (layer, i if part is None else part(word[0]), 0, 0)

    more = [] if others is None else [others]
    return pl.pallas_call(
        functools.partial(pick_kernel, flips, start),
        grid_spec=pltpu.PrefetchScalarGridSpec(
            num_scalar_prefetch=1,
            grid=(steps,),
            in_specs=[
                pl.BlockSpec((1, 1, 1, tile), block),
                pl.BlockSpec(source.shape, lambda i, word: (0, 0)),
            ]
            + [rows] * len(more),
            out_specs=rows,
        ),
        out_shape=jax.ShapeDtypeStruct((steps * tile, HALF), jnp.bfloat16),
        compiler_params=pltpu.CompilerParams(vmem_limit_bytes=VMEM),
        cost_estimate=pl.CostEstimate(
            flops=4 * steps * tile * depth * HALF,
            bytes_accessed=(steps * tile + depth) * 256,
            transcendentals=0,
        ),
    )(core, table, source, *more)


def layer_norm(values, gain):
    average = jnp.mean(values, axis=-1, keepdims=True)
    centred = values - average
    spread = jnp.mean(centred * centred, axis=-1, keepdims=True)
    return centred * lax.rsqrt(spread + 1e-05) * gain


def gelu(x):
    inner = x * (math.sqrt(2 / math.pi) + (math.sqrt(2 / math.pi) * 0.044715) * (x * x))
    half = 0.5 * x
    return half + half * jnp.tanh(inner)


def block_kernel(
    layer,
    core_ref,
    mine_ref,
    got_ref,
    qkv_a,
    qkv_b,
    out_a,
    out_b,
    up_a,
    up_b,
    down_a,
    down_b,
    gain_a,
    gain_m,
    keep_ref,
    give_ref,
    attended_ref,
    qkv_ref,
    arrived,
):
    fetch = pltpu.make_async_copy(qkv_b.at[layer], qkv_ref, arrived)
    fetch.start()
    first = core_ref[0] == 0
    mine, got = mine_ref[...], got_ref[...]
    low = jnp.where(first, mine, got)
    high = jnp.where(first, got, mine)
    current = jnp.concatenate([low, high], axis=1)
    normed = layer_norm(current.astype(jnp.float32), gain_a[layer : layer + 1]).astype(jnp.bfloat16)
    factor = math.log2(math.e) / math.sqrt(HEAD)
    over_rows = (((0,), (1,)), ((), ()))
    units = []
    for n, weight in enumerate((qkv_a.at[layer], qkv_ref)):
        if n == 1:
            fetch.wait()
        queries = lax.dot_general(
            weight[0], normed, over_rows, preferred_element_type=jnp.float32
        ).astype(jnp.bfloat16)
        keys = jnp.dot(
            normed, weight[1], preferred_element_type=jnp.float32
        ).astype(jnp.bfloat16)
        values = lax.dot_general(
            weight[2], normed, over_rows, preferred_element_type=jnp.float32
        ).astype(jnp.bfloat16)
        zero = jnp.zeros((HEAD, WIN), jnp.bfloat16)
        ones = jnp.ones((16, WIN), jnp.bfloat16)
        for h in range(2):
            rows = slice(h * HEAD, (h + 1) * HEAD)
            pair = [zero, zero]
            pair[h] = queries[rows]
            query = jnp.concatenate(pair, axis=0)
            value = jnp.concatenate([values[rows], ones], axis=0)
            for at in range(0, WIN, QUERY_TILE):
                units.append((keys, query[:, at : at + QUERY_TILE], value, n * HALF + h * HEAD, at))

    def score(unit):
        return jnp.dot(unit[0], unit[1], preferred_element_type=jnp.float32)

    def finish(unit, scores):
        top = jnp.max(scores, axis=0, keepdims=True)
        weights = jnp.exp2((scores - top) * factor).astype(jnp.bfloat16)
        sums = jnp.dot(unit[2], weights, preferred_element_type=jnp.float32)
        attended_ref[unit[3] : unit[3] + HEAD, unit[4] : unit[4] + QUERY_TILE] = (
            sums[:HEAD] / sums[HEAD : HEAD + 1]
        ).astype(jnp.bfloat16)

    ahead = score(units[0])
    for i, unit in enumerate(units):
        now, ahead = ahead, (score(units[i + 1]) if i + 1 < len(units) else None)
        finish(unit, now)
    out_weight = jnp.concatenate([out_a[layer], out_b[layer]], axis=0)
    added = lax.dot_general(
        attended_ref[...], out_weight, (((0,), (0,)), ((), ())), preferred_element_type=jnp.float32
    )
    hstream = (current.astype(jnp.float32) + added).astype(jnp.bfloat16)
    normed_two = layer_norm(hstream.astype(jnp.float32), gain_m[layer : layer + 1]).astype(jnp.bfloat16)
    parts = []
    for at in range(0, WIN, 512):
        rows = slice(at, at + 512)
        total = hstream[rows].astype(jnp.float32)
        for up, down in ((up_a, down_a), (up_b, down_b)):
            hidden = gelu(
                jnp.dot(normed_two[rows], up[layer], preferred_element_type=jnp.float32)
            )
            total = total + jnp.dot(
                hidden.astype(jnp.bfloat16), down[layer], preferred_element_type=jnp.float32
            )
        parts.append(total)
    result = jnp.concatenate(parts, axis=0)
    result = result.astype(jnp.bfloat16)
    low, high = result[:, :HALF], result[:, HALF:]
    keep_ref[...] = jnp.where(first, low, high)
    give_ref[...] = jnp.where(first, high, low)


def window_block(layer, core, mine, got, weights, gain_attn, gain_mlp):
    half = jax.ShapeDtypeStruct((WIN, HALF), jnp.bfloat16)
    whole = pl.BlockSpec(memory_space=pltpu.VMEM)
    return pl.pallas_call(
        functools.partial(block_kernel, layer),
        in_specs=[pl.BlockSpec(memory_space=pltpu.SMEM)]
        + [whole] * 3
        + [pl.BlockSpec(memory_space=pl.ANY)]
        + [whole] * len(weights),
        out_specs=[whole, whole],
        out_shape=[half, half],
        scratch_shapes=[
            pltpu.VMEM((D, WIN), jnp.bfloat16),
            pltpu.VMEM((3, D, HALF), jnp.bfloat16),
            pltpu.SemaphoreType.DMA(()),
        ],
        compiler_params=pltpu.CompilerParams(vmem_limit_bytes=VMEM),
        cost_estimate=pl.CostEstimate(
            flops=6_000_000_000, bytes_accessed=3_000_000, transcendentals=5_000_000
        ),
    )(core, mine, got, *weights, gain_attn, gain_mlp)


def shards(
    stream,
    send_rows,
    recv_slots,
    qkv_weight,
    out_weight,
    up_weight,
    down_weight,
    gain_attn,
    gain_mlp,
):
    core = lax.axis_index("ch").astype(jnp.int32)
    word = core.reshape(1)
    weights = []
    for array in (qkv_weight.transpose(0, 2, 1, 3), out_weight, up_weight, down_weight):
        weights += [array, swap(array)]
    send_table = send_rows.reshape(BLOCKS, 2, 1, -1)
    recv_table = recv_slots.reshape(BLOCKS, 2, 1, WIN)
    picked = pick(word, send_table, 0, None, stream)
    for layer in range(BLOCKS):
        moved = lax.all_to_all(
            picked.reshape(-1, 32, HALF), "pts", split_axis=0, concat_axis=0, tiled=True
        ).reshape(-1, HALF)
        got = swap(pick(word, recv_table, layer, lambda own: 1 - own, moved))
        mine = pick(word, recv_table, layer, lambda own: own, moved)
        keep, give = window_block(layer, word, mine, got, weights, gain_attn, gain_mlp)
        back = swap(give)
        if layer + 1 < BLOCKS:
            picked = pick(word, send_table, layer + 1, None, keep, flips=True)
            picked = pick(
                word, send_table, layer + 1, None, back, others=picked, start=WIN, flips=True
            )
    result = jnp.zeros((2 * WIN, HALF), jnp.bfloat16)
    result = lax.optimization_barrier(lax.dynamic_update_slice(result, keep, (core * WIN, 0)))
    return lax.dynamic_update_slice(result, back, ((1 - core) * WIN, 0))


def solution(mesh):
    in_specs = (
        P("pts", "ch"),
        P(None, "pts", None),
        P(None, "pts"),
        P(None, None, None, "ch"),
        P(None, "ch", None),
        P(None, None, "ch"),
        P(None, "ch", None),
        P(),
        P(),
    )
    out_specs = P("pts", "ch")
    return jax.shard_map(shards, mesh=mesh, in_specs=in_specs, out_specs=out_specs, check_vma=False)
```

```python
import functools
import math

import jax
import jax.numpy as jnp
from jax import lax
from jax.experimental import pallas as pl
from jax.experimental.pallas import tpu as pltpu
from jax.sharding import PartitionSpec as P

D = 256
HALF = 128
HEAD = 64
WIN = 1024
BLOCKS = 2
SWAP = [(0, 1), (1, 0)]
QUERY_TILE = 512
VMEM = 40 * 1024 * 1024


def swap(value):
    return lax.ppermute(value, "ch", SWAP)


def pick_kernel(flips, start, core_ref, index_ref, source_ref, *refs):
    out_ref = refs[-1]
    index = index_ref[0, 0]
    if flips:
        index = jnp.bitwise_xor(index, core_ref[0] * WIN)
    index = index.astype(jnp.int16)
    shape = (source_ref.shape[0], index.shape[1])
    row = lax.broadcasted_iota(jnp.int16, shape, 0) + jnp.int16(start)
    hot = jnp.where(
        jnp.broadcast_to(index, shape) == row,
        jnp.ones(shape, jnp.bfloat16),
        jnp.zeros(shape, jnp.bfloat16),
    )
    found = lax.dot_general(
        source_ref[...], hot, (((0,), (0,)), ((), ())), preferred_element_type=jnp.float32
    )
    found = found.T.astype(jnp.bfloat16)
    out_ref[...] = found if len(refs) == 1 else found + refs[0][...]


def pick(core, table, layer, part, source, others=None, start=0, flips=False):
    tile = table.shape[3]
    steps = table.shape[1] if part is None else 1
    depth = source.shape[0]
    rows = pl.BlockSpec((tile, HALF), lambda i, word: (i, 0))

    def block(i, word):
        return (layer, i if part is None else part(word[0]), 0, 0)

    more = [] if others is None else [others]
    return pl.pallas_call(
        functools.partial(pick_kernel, flips, start),
        grid_spec=pltpu.PrefetchScalarGridSpec(
            num_scalar_prefetch=1,
            grid=(steps,),
            in_specs=[
                pl.BlockSpec((1, 1, 1, tile), block),
                pl.BlockSpec(source.shape, lambda i, word: (0, 0)),
            ]
            + [rows] * len(more),
            out_specs=rows,
        ),
        out_shape=jax.ShapeDtypeStruct((steps * tile, HALF), jnp.bfloat16),
        compiler_params=pltpu.CompilerParams(vmem_limit_bytes=VMEM),
        cost_estimate=pl.CostEstimate(
            flops=4 * steps * tile * depth * HALF,
            bytes_accessed=(steps * tile + depth) * 256,
            transcendentals=0,
        ),
    )(core, table, source, *more)


def layer_norm(values, gain):
    average = jnp.mean(values, axis=-1, keepdims=True)
    centred = values - average
    spread = jnp.mean(centred * centred, axis=-1, keepdims=True)
    return centred * lax.rsqrt(spread + 1e-05) * gain


def gelu(x):
    inner = x * (math.sqrt(2 / math.pi) + (math.sqrt(2 / math.pi) * 0.044715) * (x * x))
    half = 0.5 * x
    return half + half * jnp.tanh(inner)


def block_kernel(
    layer,
    core_ref,
    mine_ref,
    got_ref,
    qkv_a,
    qkv_b,
    out_a,
    out_b,
    up_a,
    up_b,
    down_a,
    down_b,
    gain_a,
    gain_m,
    keep_ref,
    give_ref,
    attended_ref,
    qkv_ref,
    arrived,
):
    fetch = pltpu.make_async_copy(qkv_b.at[layer], qkv_ref, arrived)
    fetch.start()
    first = core_ref[0] == 0
    mine, got = mine_ref[...], got_ref[...]
    low = jnp.where(first, mine, got)
    high = jnp.where(first, got, mine)
    current = jnp.concatenate([low, high], axis=1)
    normed = layer_norm(current.astype(jnp.float32), gain_a[layer : layer + 1]).astype(jnp.bfloat16)
    factor = math.log2(math.e) / math.sqrt(HEAD)
    over_rows = (((0,), (1,)), ((), ()))
    units = []
    for n, weight in enumerate((qkv_a.at[layer], qkv_ref)):
        if n == 1:
            fetch.wait()
        queries = lax.dot_general(
            weight[0], normed, over_rows, preferred_element_type=jnp.float32
        ).astype(jnp.bfloat16)
        keys = jnp.dot(
            normed, weight[1], preferred_element_type=jnp.float32
        ).astype(jnp.bfloat16)
        values = lax.dot_general(
            weight[2], normed, over_rows, preferred_element_type=jnp.float32
        ).astype(jnp.bfloat16)
        zero = jnp.zeros((HEAD, WIN), jnp.bfloat16)
        ones = jnp.ones((16, WIN), jnp.bfloat16)
        for h in range(2):
            rows = slice(h * HEAD, (h + 1) * HEAD)
            pair = [zero, zero]
            pair[h] = queries[rows]
            query = jnp.concatenate(pair, axis=0)
            value = jnp.concatenate([values[rows], ones], axis=0)
            for at in range(0, WIN, QUERY_TILE):
                units.append((keys, query[:, at : at + QUERY_TILE], value, n * HALF + h * HEAD, at))

    def score(unit):
        return jnp.dot(unit[0], unit[1], preferred_element_type=jnp.float32)

    def finish(unit, scores):
        top = jnp.max(scores, axis=0, keepdims=True)
        weights = jnp.exp2((scores - top) * factor).astype(jnp.bfloat16)
        sums = jnp.dot(unit[2], weights, preferred_element_type=jnp.float32)
        attended_ref[unit[3] : unit[3] + HEAD, unit[4] : unit[4] + QUERY_TILE] = (
            sums[:HEAD] / sums[HEAD : HEAD + 1]
        ).astype(jnp.bfloat16)

    units.sort(key=lambda unit: unit[4])
    ahead = score(units[0])
    for i, unit in enumerate(units):
        now, ahead = ahead, (score(units[i + 1]) if i + 1 < len(units) else None)
        finish(unit, now)
    out_weight = jnp.concatenate([out_a[layer], out_b[layer]], axis=0)
    added = lax.dot_general(
        attended_ref[...], out_weight, (((0,), (0,)), ((), ())), preferred_element_type=jnp.float32
    )
    hstream = (current.astype(jnp.float32) + added).astype(jnp.bfloat16)
    normed_two = layer_norm(hstream.astype(jnp.float32), gain_m[layer : layer + 1]).astype(jnp.bfloat16)
    parts = []
    for at in range(0, WIN, 512):
        rows = slice(at, at + 512)
        total = hstream[rows].astype(jnp.float32)
        for up, down in ((up_a, down_a), (up_b, down_b)):
            hidden = gelu(
                jnp.dot(normed_two[rows], up[layer], preferred_element_type=jnp.float32)
            )
            total = total + jnp.dot(
                hidden.astype(jnp.bfloat16), down[layer], preferred_element_type=jnp.float32
            )
        parts.append(total)
    result = jnp.concatenate(parts, axis=0)
    result = result.astype(jnp.bfloat16)
    low, high = result[:, :HALF], result[:, HALF:]
    keep_ref[...] = jnp.where(first, low, high)
    give_ref[...] = jnp.where(first, high, low)


def window_block(layer, core, mine, got, weights, gain_attn, gain_mlp):
    half = jax.ShapeDtypeStruct((WIN, HALF), jnp.bfloat16)
    whole = pl.BlockSpec(memory_space=pltpu.VMEM)
    return pl.pallas_call(
        functools.partial(block_kernel, layer),
        in_specs=[pl.BlockSpec(memory_space=pltpu.SMEM)]
        + [whole] * 3
        + [pl.BlockSpec(memory_space=pl.ANY)]
        + [whole] * len(weights),
        out_specs=[whole, whole],
        out_shape=[half, half],
        scratch_shapes=[
            pltpu.VMEM((D, WIN), jnp.bfloat16),
            pltpu.VMEM((3, D, HALF), jnp.bfloat16),
            pltpu.SemaphoreType.DMA(()),
        ],
        compiler_params=pltpu.CompilerParams(vmem_limit_bytes=VMEM),
        cost_estimate=pl.CostEstimate(
            flops=6_000_000_000, bytes_accessed=3_000_000, transcendentals=5_000_000
        ),
    )(core, mine, got, *weights, gain_attn, gain_mlp)


def shards(
    stream,
    send_rows,
    recv_slots,
    qkv_weight,
    out_weight,
    up_weight,
    down_weight,
    gain_attn,
    gain_mlp,
):
    core = lax.axis_index("ch").astype(jnp.int32)
    word = core.reshape(1)
    owned = (qkv_weight.transpose(0, 2, 1, 3), out_weight, up_weight, down_weight)
    send_table = send_rows.reshape(BLOCKS, 1, 1, -1)
    recv_table = recv_slots.reshape(BLOCKS, 2, 1, WIN)
    picked = pick(word, send_table, 0, None, stream)
    for layer in range(BLOCKS):
        moved = lax.all_to_all(
            picked.reshape(-1, 32, HALF), "pts", split_axis=0, concat_axis=0, tiled=True
        ).reshape(-1, HALF)
        if layer == 0:
            moved, *owned = lax.optimization_barrier((moved, *owned))
            weights = [part for array in owned for part in (array, swap(array))]
        got = swap(pick(word, recv_table, layer, lambda own: 1 - own, moved))
        mine = pick(word, recv_table, layer, lambda own: own, moved)
        keep, give = window_block(layer, word, mine, got, weights, gain_attn, gain_mlp)
        back = swap(give)
        if layer + 1 < BLOCKS:
            picked = pick(word, send_table, layer + 1, None, keep, flips=True)
            picked = pick(
                word, send_table, layer + 1, None, back, others=picked, start=WIN, flips=True
            )
    result = jnp.zeros((2 * WIN, HALF), jnp.bfloat16)
    result = lax.optimization_barrier(lax.dynamic_update_slice(result, keep, (core * WIN, 0)))
    return lax.dynamic_update_slice(result, back, ((1 - core) * WIN, 0))


def solution(mesh):
    in_specs = (
        P("pts", "ch"),
        P(None, "pts", None),
        P(None, "pts"),
        P(None, None, None, "ch"),
        P(None, "ch", None),
        P(None, None, "ch"),
        P(None, "ch", None),
        P(),
        P(),
    )
    out_specs = P("pts", "ch")
    return jax.shard_map(shards, mesh=mesh, in_specs=in_specs, out_specs=out_specs, check_vma=False)
```

```python
import functools
import math

import jax
import jax.numpy as jnp
from jax import lax
from jax.experimental import pallas as pl
from jax.experimental.pallas import tpu as pltpu
from jax.sharding import PartitionSpec as P

D = 256
HALF = 128
HEAD = 64
WIN = 1024
BLOCKS = 2
SWAP = [(0, 1), (1, 0)]
QUERY_TILE = 512
VMEM = 40 * 1024 * 1024


def swap(value):
    return lax.ppermute(value, "ch", SWAP)


def message_order(table):
    slots, chips = table.shape
    lane = lax.broadcasted_iota(jnp.int32, table.shape, 1)
    slot = lax.broadcasted_iota(jnp.int32, table.shape, 0)
    wanted = jnp.bitwise_and(lane, slots - 1) == slot
    group = jnp.right_shift(lane, slots.bit_length() - 1)
    each = chips // slots
    parts = []
    for first in range(0, chips, each):
        spread = jnp.take_along_axis(table, group + first, axis=1, mode="promise_in_bounds")
        parts.append(jnp.sum(jnp.where(wanted, spread, 0), axis=0, keepdims=True))
    return jnp.concatenate(parts, axis=1)


def pick_kernel(flips, start, core_ref, index_ref, source_ref, *refs):
    out_ref = refs[-1]
    index = index_ref[0, 0] if len(index_ref.shape) == 4 else message_order(index_ref[0])
    if flips:
        index = jnp.bitwise_xor(index, core_ref[0] * WIN)
    index = index.astype(jnp.int16)
    shape = (source_ref.shape[0], index.shape[1])
    row = lax.broadcasted_iota(jnp.int16, shape, 0) + jnp.int16(start)
    hot = jnp.where(
        jnp.broadcast_to(index, shape) == row,
        jnp.ones(shape, jnp.bfloat16),
        jnp.zeros(shape, jnp.bfloat16),
    )
    found = lax.dot_general(
        source_ref[...], hot, (((0,), (0,)), ((), ())), preferred_element_type=jnp.float32
    )
    found = found.T.astype(jnp.bfloat16)
    out_ref[...] = found if len(refs) == 1 else found + refs[0][...]


def pick(core, table, layer, part, source, others=None, start=0, flips=False):
    tile = table.shape[3] if len(table.shape) == 4 else table.shape[1] * table.shape[2]
    depth = source.shape[0]
    rows = pl.BlockSpec((tile, HALF), lambda i, word: (i, 0))

    def block(i, word):
        return (layer, 0, 0) if part is None else (layer, part(word[0]), 0, 0)

    index_spec = pl.BlockSpec((1,) * (2 if part else 1) + table.shape[2 if part else 1 :], block)

    more = [] if others is None else [others]
    return pl.pallas_call(
        functools.partial(pick_kernel, flips, start),
        grid_spec=pltpu.PrefetchScalarGridSpec(
            num_scalar_prefetch=1,
            grid=(1,),
            in_specs=[
                index_spec,
                pl.BlockSpec(source.shape, lambda i, word: (0, 0)),
            ]
            + [rows] * len(more),
            out_specs=rows,
        ),
        out_shape=jax.ShapeDtypeStruct((tile, HALF), jnp.bfloat16),
        compiler_params=pltpu.CompilerParams(vmem_limit_bytes=VMEM),
        cost_estimate=pl.CostEstimate(
            flops=4 * tile * depth * HALF,
            bytes_accessed=(tile + depth) * 256,
            transcendentals=0,
        ),
    )(core, table, source, *more)


def layer_norm(values, gain):
    average = jnp.mean(values, axis=-1, keepdims=True)
    centred = values - average
    spread = jnp.mean(centred * centred, axis=-1, keepdims=True)
    return centred * lax.rsqrt(spread + 1e-05) * gain


def gelu(x):
    inner = x * (math.sqrt(2 / math.pi) + (math.sqrt(2 / math.pi) * 0.044715) * (x * x))
    half = 0.5 * x
    return half + half * jnp.tanh(inner)


def block_kernel(
    layer,
    core_ref,
    mine_ref,
    got_ref,
    qkv_a,
    qkv_b,
    out_a,
    out_b,
    up_a,
    up_b,
    down_a,
    down_b,
    gain_a,
    gain_m,
    keep_ref,
    give_ref,
    attended_ref,
    qkv_ref,
    arrived,
):
    fetch = pltpu.make_async_copy(qkv_b.at[layer], qkv_ref, arrived)
    fetch.start()
    first = core_ref[0] == 0
    mine, got = mine_ref[...], got_ref[...]
    low = jnp.where(first, mine, got)
    high = jnp.where(first, got, mine)
    current = jnp.concatenate([low, high], axis=1)
    normed = layer_norm(current.astype(jnp.float32), gain_a[layer : layer + 1]).astype(jnp.bfloat16)
    factor = math.log2(math.e) / math.sqrt(HEAD)
    over_rows = (((0,), (1,)), ((), ()))
    units = []
    for n, weight in enumerate((qkv_a.at[layer], qkv_ref)):
        if n == 1:
            fetch.wait()
        queries = lax.dot_general(
            weight[0], normed, over_rows, preferred_element_type=jnp.float32
        ).astype(jnp.bfloat16)
        keys = jnp.dot(
            normed, weight[1], preferred_element_type=jnp.float32
        ).astype(jnp.bfloat16)
        values = lax.dot_general(
            weight[2], normed, over_rows, preferred_element_type=jnp.float32
        ).astype(jnp.bfloat16)
        zero = jnp.zeros((HEAD, WIN), jnp.bfloat16)
        ones = jnp.ones((16, WIN), jnp.bfloat16)
        for h in range(2):
            rows = slice(h * HEAD, (h + 1) * HEAD)
            pair = [zero, zero]
            pair[h] = queries[rows]
            query = jnp.concatenate(pair, axis=0)
            value = jnp.concatenate([values[rows], ones], axis=0)
            for at in range(0, WIN, QUERY_TILE):
                units.append((keys, query[:, at : at + QUERY_TILE], value, n * HALF + h * HEAD, at))

    def score(unit):
        return jnp.dot(unit[0], unit[1], preferred_element_type=jnp.float32)

    def finish(unit, scores):
        top = jnp.max(scores, axis=0, keepdims=True)
        weights = jnp.exp2((scores - top) * factor).astype(jnp.bfloat16)
        sums = jnp.dot(unit[2], weights, preferred_element_type=jnp.float32)
        attended_ref[unit[3] : unit[3] + HEAD, unit[4] : unit[4] + QUERY_TILE] = (
            sums[:HEAD] / sums[HEAD : HEAD + 1]
        ).astype(jnp.bfloat16)

    units.sort(key=lambda unit: unit[4])
    ahead = score(units[0])
    for i, unit in enumerate(units):
        now, ahead = ahead, (score(units[i + 1]) if i + 1 < len(units) else None)
        finish(unit, now)
    out_weight = jnp.concatenate([out_a[layer], out_b[layer]], axis=0)
    added = lax.dot_general(
        attended_ref[...], out_weight, (((0,), (0,)), ((), ())), preferred_element_type=jnp.float32
    )
    hstream = (current.astype(jnp.float32) + added).astype(jnp.bfloat16)
    normed_two = layer_norm(hstream.astype(jnp.float32), gain_m[layer : layer + 1]).astype(jnp.bfloat16)
    parts = []
    for at in range(0, WIN, 512):
        rows = slice(at, at + 512)
        total = hstream[rows].astype(jnp.float32)
        for up, down in ((up_a, down_a), (up_b, down_b)):
            hidden = gelu(
                jnp.dot(normed_two[rows], up[layer], preferred_element_type=jnp.float32)
            )
            total = total + jnp.dot(
                hidden.astype(jnp.bfloat16), down[layer], preferred_element_type=jnp.float32
            )
        parts.append(total)
    result = jnp.concatenate(parts, axis=0)
    result = result.astype(jnp.bfloat16)
    low, high = result[:, :HALF], result[:, HALF:]
    keep_ref[...] = jnp.where(first, low, high)
    give_ref[...] = jnp.where(first, high, low)


def window_block(layer, core, mine, got, weights, gain_attn, gain_mlp):
    half = jax.ShapeDtypeStruct((WIN, HALF), jnp.bfloat16)
    whole = pl.BlockSpec(memory_space=pltpu.VMEM)
    return pl.pallas_call(
        functools.partial(block_kernel, layer),
        in_specs=[pl.BlockSpec(memory_space=pltpu.SMEM)]
        + [whole] * 3
        + [pl.BlockSpec(memory_space=pl.ANY)]
        + [whole] * len(weights),
        out_specs=[whole, whole],
        out_shape=[half, half],
        scratch_shapes=[
            pltpu.VMEM((D, WIN), jnp.bfloat16),
            pltpu.VMEM((3, D, HALF), jnp.bfloat16),
            pltpu.SemaphoreType.DMA(()),
        ],
        compiler_params=pltpu.CompilerParams(vmem_limit_bytes=VMEM),
        cost_estimate=pl.CostEstimate(
            flops=6_000_000_000, bytes_accessed=3_000_000, transcendentals=5_000_000
        ),
    )(core, mine, got, *weights, gain_attn, gain_mlp)


def shards(
    stream,
    send_rows,
    recv_slots,
    qkv_weight,
    out_weight,
    up_weight,
    down_weight,
    gain_attn,
    gain_mlp,
):
    core = lax.axis_index("ch").astype(jnp.int32)
    word = core.reshape(1)
    owned = (qkv_weight.transpose(0, 2, 1, 3), out_weight, up_weight, down_weight)
    send_table = send_rows.transpose(0, 2, 1)
    recv_table = recv_slots.reshape(BLOCKS, 2, 1, WIN)
    picked = pick(word, send_table, 0, None, stream)
    for layer in range(BLOCKS):
        moved = lax.all_to_all(
            picked.reshape(-1, 32, HALF), "pts", split_axis=0, concat_axis=0, tiled=True
        ).reshape(-1, HALF)
        if layer == 0:
            moved, *owned = lax.optimization_barrier((moved, *owned))
            weights = [part for array in owned for part in (array, swap(array))]
        got = swap(pick(word, recv_table, layer, lambda own: 1 - own, moved))
        mine = pick(word, recv_table, layer, lambda own: own, moved)
        keep, give = window_block(layer, word, mine, got, weights, gain_attn, gain_mlp)
        back = swap(give)
        if layer + 1 < BLOCKS:
            picked = pick(word, send_table, layer + 1, None, keep, flips=True)
            picked = pick(
                word, send_table, layer + 1, None, back, others=picked, start=WIN, flips=True
            )
    result = jnp.zeros((2 * WIN, HALF), jnp.bfloat16)
    result = lax.optimization_barrier(lax.dynamic_update_slice(result, keep, (core * WIN, 0)))
    return lax.dynamic_update_slice(result, back, ((1 - core) * WIN, 0))


def solution(mesh):
    in_specs = (
        P("pts", "ch"),
        P(None, "pts", None),
        P(None, "pts"),
        P(None, None, None, "ch"),
        P(None, "ch", None),
        P(None, None, "ch"),
        P(None, "ch", None),
        P(),
        P(),
    )
    out_specs = P("pts", "ch")
    return jax.shard_map(shards, mesh=mesh, in_specs=in_specs, out_specs=out_specs, check_vma=False)
```

```python
import functools
import math

import jax
import jax.numpy as jnp
from jax import lax
from jax.experimental import pallas as pl
from jax.experimental.pallas import tpu as pltpu
from jax.sharding import PartitionSpec as P

D = 256
HALF = 128
HEAD = 64
WIN = 1024
BLOCKS = 2
SWAP = [(0, 1), (1, 0)]
QUERY_TILE = 512
VMEM = 40 * 1024 * 1024


def swap(value):
    return lax.ppermute(value, "ch", SWAP)


def pick_kernel(flips, start, core_ref, index_ref, source_ref, *refs):
    out_ref = refs[-1]
    index = index_ref[0, 0]
    if flips:
        index = jnp.bitwise_xor(index, core_ref[0] * WIN)
    index = index.astype(jnp.int16)
    shape = (source_ref.shape[0], index.shape[1])
    row = lax.broadcasted_iota(jnp.int16, shape, 0) + jnp.int16(start)
    hot = jnp.where(
        jnp.broadcast_to(index, shape) == row,
        jnp.ones(shape, jnp.bfloat16),
        jnp.zeros(shape, jnp.bfloat16),
    )
    found = lax.dot_general(
        source_ref[...], hot, (((0,), (0,)), ((), ())), preferred_element_type=jnp.float32
    )
    found = found.T.astype(jnp.bfloat16)
    out_ref[...] = found if len(refs) == 1 else found + refs[0][...]


def pick(core, table, layer, part, source, others=None, start=0, flips=False):
    tile = table.shape[3]
    steps = table.shape[1] if part is None else 1
    depth = source.shape[0]
    rows = pl.BlockSpec((tile, HALF), lambda i, word: (i, 0))

    def block(i, word):
        return (layer, i if part is None else part(word[0]), 0, 0)

    more = [] if others is None else [others]
    return pl.pallas_call(
        functools.partial(pick_kernel, flips, start),
        grid_spec=pltpu.PrefetchScalarGridSpec(
            num_scalar_prefetch=1,
            grid=(steps,),
            in_specs=[
                pl.BlockSpec((1, 1, 1, tile), block),
                pl.BlockSpec(source.shape, lambda i, word: (0, 0)),
            ]
            + [rows] * len(more),
            out_specs=rows,
        ),
        out_shape=jax.ShapeDtypeStruct((steps * tile, HALF), jnp.bfloat16),
        compiler_params=pltpu.CompilerParams(vmem_limit_bytes=VMEM),
        cost_estimate=pl.CostEstimate(
            flops=4 * steps * tile * depth * HALF,
            bytes_accessed=(steps * tile + depth) * 256,
            transcendentals=0,
        ),
    )(core, table, source, *more)


def first_pick_kernel(index_ref, stream_ref, out_ref, held, arrived):
    copies = [
        pltpu.make_async_copy(stream_ref.at[pl.ds(k * WIN, WIN)], held.at[k], arrived.at[k])
        for k in range(2)
    ]
    for copy in copies:
        copy.start()
    index = index_ref[0, 0].astype(jnp.int16)
    shape = (WIN, index.shape[1])
    total = None
    for k, copy in enumerate(copies):
        row = lax.broadcasted_iota(jnp.int16, shape, 0) + jnp.int16(k * WIN)
        hot = jnp.where(
            jnp.broadcast_to(index, shape) == row,
            jnp.ones(shape, jnp.bfloat16),
            jnp.zeros(shape, jnp.bfloat16),
        )
        copy.wait()
        part = lax.dot_general(
            held[k], hot, (((0,), (0,)), ((), ())), preferred_element_type=jnp.float32
        )
        total = part if total is None else total + part
    out_ref[...] = total.T.astype(jnp.bfloat16)


def first_pick(table, stream):
    tile = table.shape[3]
    return pl.pallas_call(
        first_pick_kernel,
        grid=(1,),
        in_specs=[
            pl.BlockSpec((1, 1, 1, tile), lambda i: (0, 0, 0, 0)),
            pl.BlockSpec(memory_space=pltpu.HBM),
        ],
        out_specs=pl.BlockSpec((tile, HALF), lambda i: (0, 0)),
        out_shape=jax.ShapeDtypeStruct((tile, HALF), jnp.bfloat16),
        scratch_shapes=[
            pltpu.VMEM((2, WIN, HALF), jnp.bfloat16),
            pltpu.SemaphoreType.DMA((2,)),
        ],
        compiler_params=pltpu.CompilerParams(vmem_limit_bytes=60 * 1024 * 1024),
        cost_estimate=pl.CostEstimate(
            flops=8 * tile * WIN * HALF, bytes_accessed=tile * 384, transcendentals=0
        ),
    )(table, stream)


def layer_norm(values, gain):
    average = jnp.mean(values, axis=-1, keepdims=True)
    centred = values - average
    spread = jnp.mean(centred * centred, axis=-1, keepdims=True)
    return centred * lax.rsqrt(spread + 1e-05) * gain


def gelu(x):
    inner = x * (math.sqrt(2 / math.pi) + (math.sqrt(2 / math.pi) * 0.044715) * (x * x))
    half = 0.5 * x
    return half + half * jnp.tanh(inner)


def block_kernel(
    layer,
    core_ref,
    mine_ref,
    got_ref,
    qkv_a,
    qkv_b,
    out_a,
    out_b,
    up_a,
    up_b,
    down_a,
    down_b,
    gain_a,
    gain_m,
    keep_ref,
    give_ref,
    attended_ref,
    qkv_ref,
    arrived,
):
    fetch = pltpu.make_async_copy(qkv_b.at[layer], qkv_ref, arrived)
    fetch.start()
    first = core_ref[0] == 0
    mine, got = mine_ref[...], got_ref[...]
    low = jnp.where(first, mine, got)
    high = jnp.where(first, got, mine)
    current = jnp.concatenate([low, high], axis=1)
    normed = layer_norm(current.astype(jnp.float32), gain_a[layer : layer + 1]).astype(jnp.bfloat16)
    factor = math.log2(math.e) / math.sqrt(HEAD)
    over_rows = (((0,), (1,)), ((), ()))
    units = []
    for n, weight in enumerate((qkv_a.at[layer], qkv_ref)):
        if n == 1:
            fetch.wait()
        queries = lax.dot_general(
            weight[0], normed, over_rows, preferred_element_type=jnp.float32
        ).astype(jnp.bfloat16)
        keys = jnp.dot(
            normed, weight[1], preferred_element_type=jnp.float32
        ).astype(jnp.bfloat16)
        values = lax.dot_general(
            weight[2], normed, over_rows, preferred_element_type=jnp.float32
        ).astype(jnp.bfloat16)
        zero = jnp.zeros((HEAD, WIN), jnp.bfloat16)
        ones = jnp.ones((16, WIN), jnp.bfloat16)
        for h in range(2):
            rows = slice(h * HEAD, (h + 1) * HEAD)
            pair = [zero, zero]
            pair[h] = queries[rows]
            query = jnp.concatenate(pair, axis=0)
            value = jnp.concatenate([values[rows], ones], axis=0)
            for at in range(0, WIN, QUERY_TILE):
                units.append((keys, query[:, at : at + QUERY_TILE], value, n * HALF + h * HEAD, at))

    def score(unit):
        return jnp.dot(unit[0], unit[1], preferred_element_type=jnp.float32)

    def finish(unit, scores):
        top = jnp.max(scores, axis=0, keepdims=True)
        weights = jnp.exp2((scores - top) * factor).astype(jnp.bfloat16)
        sums = jnp.dot(unit[2], weights, preferred_element_type=jnp.float32)
        attended_ref[unit[3] : unit[3] + HEAD, unit[4] : unit[4] + QUERY_TILE] = (
            sums[:HEAD] / sums[HEAD : HEAD + 1]
        ).astype(jnp.bfloat16)

    units.sort(key=lambda unit: unit[4])
    ahead = score(units[0])
    for i, unit in enumerate(units):
        now, ahead = ahead, (score(units[i + 1]) if i + 1 < len(units) else None)
        finish(unit, now)
    out_weight = jnp.concatenate([out_a[layer], out_b[layer]], axis=0)
    added = lax.dot_general(
        attended_ref[...], out_weight, (((0,), (0,)), ((), ())), preferred_element_type=jnp.float32
    )
    hstream = (current.astype(jnp.float32) + added).astype(jnp.bfloat16)
    normed_two = layer_norm(hstream.astype(jnp.float32), gain_m[layer : layer + 1]).astype(jnp.bfloat16)
    parts = []
    for at in range(0, WIN, 512):
        rows = slice(at, at + 512)
        total = hstream[rows].astype(jnp.float32)
        for up, down in ((up_a, down_a), (up_b, down_b)):
            hidden = gelu(
                jnp.dot(normed_two[rows], up[layer], preferred_element_type=jnp.float32)
            )
            total = total + jnp.dot(
                hidden.astype(jnp.bfloat16), down[layer], preferred_element_type=jnp.float32
            )
        parts.append(total)
    result = jnp.concatenate(parts, axis=0)
    result = result.astype(jnp.bfloat16)
    low, high = result[:, :HALF], result[:, HALF:]
    keep_ref[...] = jnp.where(first, low, high)
    give_ref[...] = jnp.where(first, high, low)


def window_block(layer, core, mine, got, weights, gain_attn, gain_mlp):
    half = jax.ShapeDtypeStruct((WIN, HALF), jnp.bfloat16)
    whole = pl.BlockSpec(memory_space=pltpu.VMEM)
    return pl.pallas_call(
        functools.partial(block_kernel, layer),
        in_specs=[pl.BlockSpec(memory_space=pltpu.SMEM)]
        + [whole] * 3
        + [pl.BlockSpec(memory_space=pl.ANY)]
        + [whole] * len(weights),
        out_specs=[whole, whole],
        out_shape=[half, half],
        scratch_shapes=[
            pltpu.VMEM((D, WIN), jnp.bfloat16),
            pltpu.VMEM((3, D, HALF), jnp.bfloat16),
            pltpu.SemaphoreType.DMA(()),
        ],
        compiler_params=pltpu.CompilerParams(vmem_limit_bytes=VMEM),
        cost_estimate=pl.CostEstimate(
            flops=6_000_000_000, bytes_accessed=3_000_000, transcendentals=5_000_000
        ),
    )(core, mine, got, *weights, gain_attn, gain_mlp)


def shards(
    stream,
    send_rows,
    recv_slots,
    qkv_weight,
    out_weight,
    up_weight,
    down_weight,
    gain_attn,
    gain_mlp,
):
    core = lax.axis_index("ch").astype(jnp.int32)
    word = core.reshape(1)
    owned = (qkv_weight.transpose(0, 2, 1, 3), out_weight, up_weight, down_weight)
    send_table = send_rows.reshape(BLOCKS, 1, 1, -1)
    recv_table = recv_slots.reshape(BLOCKS, 2, 1, WIN)
    picked = first_pick(send_table, stream)
    for layer in range(BLOCKS):
        moved = lax.all_to_all(
            picked.reshape(-1, 32, HALF), "pts", split_axis=0, concat_axis=0, tiled=True
        ).reshape(-1, HALF)
        if layer == 0:
            moved, *owned = lax.optimization_barrier((moved, *owned))
            weights = [part for array in owned for part in (array, swap(array))]
        got = swap(pick(word, recv_table, layer, lambda own: 1 - own, moved))
        mine = pick(word, recv_table, layer, lambda own: own, moved)
        keep, give = window_block(layer, word, mine, got, weights, gain_attn, gain_mlp)
        back = swap(give)
        if layer + 1 < BLOCKS:
            picked = pick(word, send_table, layer + 1, None, keep, flips=True)
            picked = pick(
                word, send_table, layer + 1, None, back, others=picked, start=WIN, flips=True
            )
    result = jnp.zeros((2 * WIN, HALF), jnp.bfloat16)
    result = lax.optimization_barrier(lax.dynamic_update_slice(result, keep, (core * WIN, 0)))
    return lax.dynamic_update_slice(result, back, ((1 - core) * WIN, 0))


def solution(mesh):
    in_specs = (
        P("pts", "ch"),
        P(None, "pts", None),
        P(None, "pts"),
        P(None, None, None, "ch"),
        P(None, "ch", None),
        P(None, None, "ch"),
        P(None, "ch", None),
        P(),
        P(),
    )
    out_specs = P("pts", "ch")
    return jax.shard_map(shards, mesh=mesh, in_specs=in_specs, out_specs=out_specs, check_vma=False)
```
